32 devices in a mesh: replica: 8 (over z, core), tensor: 4 (over y, x).
Axes of the slice: x: 2, y: 2, z: 4, core: 2. Of those that a mesh axis runs over, the one named last changes fastest.
Arguments:
- token_ids: int32 [768, 4], P('replica'), may hold values from 0 to 32063, as said below
- cache_lengths: int32 [768], P('replica'), may hold values from 2 to 160, as said below
- embedding: bfloat16 [32064, 8192], P('replica', 'tensor'), may hold values from -15 to 15
- norm_gain: float32 [8192], replicated, may hold values from 0.5 to 1.5
- rotated_key_cache: bfloat16 [768, 160, 1024], P('replica', None, 'tensor'), may hold values from -200 to 200
- stored_value_cache: bfloat16 [768, 160, 1024], P('replica', None, 'tensor'), may hold values from -6 to 6
- teacher_q: float32 [8192, 4096], P(('replica', 'tensor')), may hold values from -0.0625 to 0.0625
- teacher_k: float32 [8192, 1024], P(('replica', 'tensor')), may hold values from -0.0625 to 0.0625
- teacher_v: float32 [8192, 1024], P(('replica', 'tensor')), may hold values from -0.0625 to 0.0625
- teacher_o: float32 [8192, 4096], P(('replica', 'tensor')), may hold values from -0.09375 to 0.09375
- student_q: float32 [8192, 4096], P(('replica', 'tensor')), may hold values from -0.0625 to 0.0625
- student_k: float32 [8192, 1024], P(('replica', 'tensor')), may hold values from -0.0625 to 0.0625
- student_v: float32 [8192, 1024], P(('replica', 'tensor')), may hold values from -0.0625 to 0.0625
- student_o: float32 [8192, 4096], P(('replica', 'tensor')), may hold values from -0.09375 to 0.09375
Outputs:
- next_q: float32 [8192, 4096], P(('replica', 'tensor'))
- next_k: float32 [8192, 1024], P(('replica', 'tensor'))
- next_v: float32 [8192, 1024], P(('replica', 'tensor'))
- next_o: float32 [8192, 4096], P(('replica', 'tensor'))
- hidden_out: bfloat16 [768, 4, 8192], P('replica', None, 'tensor')
The draws below stay inside these ranges and needn't reach their ends.
Inputs may be any that keep to these rules, and one draw needn't show every extreme that they name: `token_ids`: the 384 ids of one replica's rows fall at most 96 times into one block of 4008 consecutive vocabulary entries, and exactly 96 times into one such block. `cache_lengths`: filled cache slots of a row; slots from it on hold nothing that is read.
All inputs are finite; a program needn't handle non-finite values.
Results may differ from the reference program's by a relative error of at most 0.0076.
Values may be sent and summed in bfloat16 or wider, within the bound.
No kernel may reach another device: no remote copies, remote signals or barrier semaphores. Data moves between devices by JAX's collectives and lax.ppermute only.
A program may use at most 256 MiB of HBM per device.

```python
import jax
import jax.numpy as jnp
from jax import lax

D = 8192
QUERY_HEADS = 32
KEY_VALUE_HEADS = 8
HEAD_WIDTH = 128
V_SHARD = 4008
ROWS_REP = 96
CACHE_SLOTS = 160
DECODE_STEPS = 4
QD = 4096
KD = 1024
VOCAB = 32064
DECODE_ROWS = 768


def draw_embedding(key, part):
    key = jax.random.fold_in(key, 11)
    base_key, scale_key = jax.random.split(key)
    base = jnp.clip(jax.random.normal(base_key, (VOCAB, D), jnp.float32), -5.0, 5.0)
    row_scale = jnp.exp(jax.random.uniform(scale_key, (VOCAB, 1), jnp.float32, jnp.log(0.3), jnp.log(3.0)))
    return (base * row_scale).astype(jnp.bfloat16)


def draw_rotated_key_cache(key, part):
    key = jax.random.fold_in(key, 12)
    base_key = jax.random.fold_in(key, 0)
    base = jnp.clip(jax.random.normal(base_key, (DECODE_ROWS, CACHE_SLOTS, KD), jnp.float32), -5.0, 5.0)
    return base.astype(jnp.bfloat16)


def draw_cache_lengths(key, part):
    key = jax.random.fold_in(key, 13)
    length_key, pick_key = jax.random.split(key)
    filled = jax.random.randint(length_key, (DECODE_ROWS,), 2, CACHE_SLOTS + 1, dtype=jnp.int32)
    chosen = jax.random.randint(pick_key, (), 0, DECODE_ROWS, dtype=jnp.int32)
    return jnp.where(jnp.arange(DECODE_ROWS, dtype=jnp.int32) == chosen, CACHE_SLOTS, filled).astype(jnp.int32)


def draw_token_ids(key, part):
    key = jax.random.fold_in(key, 14)
    shard_count = VOCAB // V_SHARD
    replica_slots = ROWS_REP * DECODE_STEPS
    capacity = 2 * replica_slots // shard_count
    first_key, order_key, entry_key = jax.random.split(key, 3)
    full_shard = jax.random.randint(first_key, (shard_count, 1), 0, shard_count, dtype=jnp.int32)
    slot_index = jnp.arange(replica_slots, dtype=jnp.int32)[None, :]
    spread = (full_shard + 1 + (slot_index - capacity) % (shard_count - 1)) % shard_count
    owners = jnp.where(slot_index < capacity, full_shard, spread).astype(jnp.int32)
    order_keys = jax.random.split(order_key, shard_count)
    orders = jax.vmap(lambda one_key: jax.random.permutation(one_key, replica_slots))(order_keys).astype(jnp.int32)
    shuffled = jnp.take_along_axis(owners, orders, axis=1)
    entries = jax.random.randint(entry_key, (shard_count, replica_slots), 0, V_SHARD, dtype=jnp.int32)
    ids = shuffled * V_SHARD + entries
    return ids.reshape(DECODE_ROWS, DECODE_STEPS).astype(jnp.int32)


def level_of(key, dims, cuts, smallest, top_value):
    def one(axis_at, blocks):
        heights = jax.random.uniform(jax.random.fold_in(jax.random.fold_in(key, 6), axis_at), (blocks,), jnp.float32, smallest / len(cuts), top_value / len(cuts))
        return jnp.repeat(jnp.exp(heights), dims[axis_at] // blocks).reshape((-1,) + (1,) * (len(dims) - axis_at - 1))

    gain = one(*cuts[0])
    for cut in cuts[1:]:
        gain = gain * one(*cut)
    return gain


def normal_values(stream_key, shape, width, most, cuts=(), kind=jnp.bfloat16):
    drawn = jax.random.normal(stream_key, shape, jnp.float32) * width
    if len(cuts) > 0:
        drawn = level_of(stream_key, shape, cuts, -0.22, 0.18) * drawn
    return jnp.clip(drawn, min=-most, max=most).astype(kind)


def setup_inputs(seed: int = 0) -> dict:
    streams_of = jax.random.split(jax.random.key(seed), 15)
    token_ids = draw_token_ids(jax.random.fold_in(streams_of[14], 71), 0)
    cache_lengths = draw_cache_lengths(jax.random.fold_in(streams_of[14], 71), 0)
    embedding = draw_embedding(jax.random.fold_in(streams_of[14], 71), 0)
    norm_gain = jnp.clip(1.0 + 0.1 * jax.random.normal(streams_of[3], (D,), jnp.float32), 0.5, 1.5)
    rotated_key_cache = draw_rotated_key_cache(jax.random.fold_in(streams_of[14], 71), 0)
    stored_value_cache = normal_values(streams_of[5], (DECODE_ROWS, CACHE_SLOTS, KD), 1.0, 6.0, ((0, 8), (2, 4)))
    teacher_q = normal_values(streams_of[6], (D, QD), D ** -0.5, 0.0625, ((0, 32),), jnp.float32)
    teacher_k = normal_values(streams_of[7], (D, KD), D ** -0.5, 0.0625, ((0, 32),), jnp.float32)
    teacher_v = normal_values(streams_of[8], (D, KD), D ** -0.5, 0.0625, ((0, 32),), jnp.float32)
    teacher_o = normal_values(streams_of[9], (D, QD), QD ** -0.5, 0.09375, ((0, 32),), jnp.float32)
    student_q = normal_values(streams_of[10], (D, QD), D ** -0.5, 0.0625, ((0, 32),), jnp.float32)
    student_k = normal_values(streams_of[11], (D, KD), D ** -0.5, 0.0625, ((0, 32),), jnp.float32)
    student_v = normal_values(streams_of[12], (D, KD), D ** -0.5, 0.0625, ((0, 32),), jnp.float32)
    student_o = normal_values(streams_of[13], (D, QD), QD ** -0.5, 0.09375, ((0, 32),), jnp.float32)
    return dict(token_ids=token_ids, cache_lengths=cache_lengths, embedding=embedding, norm_gain=norm_gain, rotated_key_cache=rotated_key_cache, stored_value_cache=stored_value_cache, teacher_q=teacher_q, teacher_k=teacher_k, teacher_v=teacher_v, teacher_o=teacher_o, student_q=student_q, student_k=student_k, student_v=student_v, student_o=student_o)


blend_keep = 0.9
norm_epsilon = 1e-05
rope_theta = 500000.0
masked_score = -1e+30

def rotate_half(values, cosine_table, sine_table):
    half_width = values.shape[-1] // 2
    first_half = values[..., :half_width]
    second_half = values[..., half_width:]
    return jnp.concatenate([first_half * cosine_table - second_half * sine_table, second_half * cosine_table + first_half * sine_table], axis=-1)

def reference(token_ids, cache_lengths, embedding, norm_gain, rotated_key_cache, stored_value_cache, teacher_q, teacher_k, teacher_v, teacher_o, student_q, student_k, student_v, student_o):
    next_q = blend_keep * teacher_q + (1.0 - blend_keep) * student_q
    next_k = blend_keep * teacher_k + (1.0 - blend_keep) * student_k
    next_v = blend_keep * teacher_v + (1.0 - blend_keep) * student_v
    next_o = blend_keep * teacher_o + (1.0 - blend_keep) * student_o
    sampler_q = next_q.astype(jnp.bfloat16)
    sampler_key_weight = next_k.astype(jnp.bfloat16)
    sampler_value_weight = next_v.astype(jnp.bfloat16)
    sampler_o = next_o.astype(jnp.bfloat16)
    tokens = jnp.take(embedding, token_ids, axis=0)
    widened = tokens.astype(jnp.float32)
    mean_square = lax.optimization_barrier(jnp.mean(widened * widened, axis=-1, keepdims=True))
    normed = (widened * lax.rsqrt(mean_square + norm_epsilon) * norm_gain).astype(jnp.bfloat16)
    flattened_rows = normed.reshape(DECODE_ROWS * DECODE_STEPS, D)
    positions = (cache_lengths[:, None] + jnp.arange(DECODE_STEPS, dtype=jnp.int32)[None, :]).astype(jnp.float32)
    inverse = rope_theta ** (-(jnp.arange(HEAD_WIDTH // 2, dtype=jnp.float32) * 2.0) / HEAD_WIDTH)
    angles = positions[:, :, None] * inverse
    cosine_table = jnp.cos(angles)[:, :, None, :]
    sine_table = jnp.sin(angles)[:, :, None, :]
    query_rows = jnp.dot(flattened_rows, sampler_q, preferred_element_type=jnp.float32).reshape(DECODE_ROWS, DECODE_STEPS, QUERY_HEADS, HEAD_WIDTH)
    query_rows = rotate_half(query_rows, cosine_table, sine_table).astype(jnp.bfloat16)
    incoming_keys = jnp.dot(flattened_rows, sampler_key_weight, preferred_element_type=jnp.float32).reshape(DECODE_ROWS, DECODE_STEPS, KEY_VALUE_HEADS, HEAD_WIDTH)
    incoming_keys = rotate_half(incoming_keys, cosine_table, sine_table).astype(jnp.bfloat16)
    incoming_values = jnp.dot(flattened_rows, sampler_value_weight, preferred_element_type=jnp.float32).astype(jnp.bfloat16).reshape(DECODE_ROWS, DECODE_STEPS, KEY_VALUE_HEADS, HEAD_WIDTH)
    query_group_width = QUERY_HEADS // KEY_VALUE_HEADS
    score_scale = HEAD_WIDTH ** (-0.5)
    grouped_queries = query_rows.reshape(DECODE_ROWS, DECODE_STEPS, KEY_VALUE_HEADS, query_group_width, HEAD_WIDTH).astype(jnp.float32)
    cached_key_rows = rotated_key_cache.reshape(DECODE_ROWS, CACHE_SLOTS, KEY_VALUE_HEADS, HEAD_WIDTH).astype(jnp.float32)
    cached_value_rows = stored_value_cache.reshape(DECODE_ROWS, CACHE_SLOTS, KEY_VALUE_HEADS, HEAD_WIDTH).astype(jnp.float32)
    cache_scores = jnp.einsum('rsgqd,rcgd->rsgqc', grouped_queries, cached_key_rows) * score_scale
    cache_valid = jnp.arange(CACHE_SLOTS, dtype=jnp.int32)[None, :] < cache_lengths[:, None]
    cache_scores = jnp.where(cache_valid[:, None, None, None, :], cache_scores, masked_score)
    fresh_scores = jnp.einsum('rsgqd,rtgd->rsgqt', grouped_queries, incoming_keys.astype(jnp.float32)) * score_scale
    fresh_valid = jnp.arange(DECODE_STEPS, dtype=jnp.int32)[None, :] <= jnp.arange(DECODE_STEPS, dtype=jnp.int32)[:, None]
    fresh_scores = jnp.where(fresh_valid[None, :, None, None, :], fresh_scores, masked_score)
    highest = jnp.maximum(lax.optimization_barrier(jnp.max(cache_scores, axis=-1)), lax.optimization_barrier(jnp.max(fresh_scores, axis=-1)))[..., None]
    cache_exp = jnp.exp(cache_scores - highest)
    fresh_exp = jnp.exp(fresh_scores - highest)
    totals = (lax.optimization_barrier(jnp.sum(cache_exp, axis=-1)) + lax.optimization_barrier(jnp.sum(fresh_exp, axis=-1)))[..., None]
    cache_probs = (cache_exp / totals).astype(jnp.bfloat16).astype(jnp.float32)
    fresh_probs = (fresh_exp / totals).astype(jnp.bfloat16).astype(jnp.float32)
    attended = jnp.einsum('rsgqc,rcgd->rsgqd', cache_probs, cached_value_rows) + jnp.einsum('rsgqt,rtgd->rsgqd', fresh_probs, incoming_values.astype(jnp.float32))
    attended = attended.astype(jnp.bfloat16).reshape(DECODE_ROWS * DECODE_STEPS, QD)
    projected = jnp.dot(attended, sampler_o.T, preferred_element_type=jnp.float32).reshape(DECODE_ROWS, DECODE_STEPS, D)
    hidden_out = (widened + projected).astype(jnp.bfloat16)
    return (next_q, next_k, next_v, next_o, hidden_out)
```

```python
import functools

import jax
import jax.numpy as jnp
import numpy as np
from jax import lax
from jax.experimental import pallas as pl
from jax.experimental.pallas import tpu as pltpu
from jax.sharding import PartitionSpec as P

D = 8192
HEAD_WIDTH = 128
DECODE_STEPS = 4
CORES = 2

blend_keep = 0.9
norm_epsilon = 1e-05
rope_theta = 500000.0
masked_score = -1e30

VMEM = 60 * 1024 * 1024

f32 = jnp.float32
bf16 = jnp.bfloat16


def swap(values, bits, count):
    return lax.ppermute(values, "tensor", [(i, i ^ bits) for i in range(count)])


def pass_kernel(values_ref, other_ref, out_ref):
    pass


def after(values, other):
    anywhere = pl.BlockSpec(memory_space=pl.ANY)
    return pl.pallas_call(
        pass_kernel,
        in_specs=[anywhere, anywhere],
        out_specs=anywhere,
        out_shape=jax.ShapeDtypeStruct(values.shape, values.dtype),
        input_output_aliases={0: 0},
        cost_estimate=pl.CostEstimate(flops=0, bytes_accessed=0, transcendentals=0),
    )(values, other)


def due_order(count):
    if count == 4:
        order = [[3, 2, 1, 0], [0, 3, 2, 1], [3, 0, 1, 2], [0, 1, 2, 3]]
    else:
        order = [
            sorted(range(count), key=lambda d, z=z: (d == z, -abs(d - z))) for z in range(count)
        ]
    return np.array(order, dtype=np.int32)


def line_sum(products, place, count, gates):
    if count == 4:
        first, second, third, own = products
        one = lax.ppermute(first, "z", [(0, 1), (3, 2)])
        one = after(one, gates[0])
        block = (second.astype(f32) + one.astype(f32)).astype(bf16)
        up = lax.ppermute(block, "z", [(0, 1), (1, 2)])
        down = lax.ppermute(block, "z", [(3, 2), (2, 1)])
        up = after(up, gates[1])
        rest = jnp.where(place == 2, first, third).astype(f32)
        block = (rest + up.astype(f32)).astype(bf16)
        up = lax.ppermute(block, "z", [(0, 1), (1, 2), (2, 3)])
        rest = jnp.where(place == 1, first, third).astype(f32)
        block = (rest + down.astype(f32)).astype(bf16)
        down = lax.ppermute(block, "z", [(3, 2), (2, 1), (1, 0)])
        return own, up, down
    order = due_order(count)
    arrived = [None, None]
    for step in range(1, count):
        for way, sign in enumerate((1, -1)):
            sources = [z for z in range(count) if 0 <= z + sign * (count - step) < count]
            picks = {z: int(np.where(order[z] == z + sign * (count - step))[0][0]) for z in sources}
            names = sorted(set(picks.values()))
            block = products[names[0]].astype(f32)
            for name in names[1:]:
                chosen = functools.reduce(
                    jnp.logical_or, [place == z for z in sources if picks[z] == name]
                )
                block = jnp.where(chosen, products[name].astype(f32), block)
            if arrived[way] is not None:
                block = block + arrived[way].astype(f32)
            pairs = [(z, z + sign) for z in sources if 0 <= z + sign < count]
            arrived[way] = lax.ppermute(block.astype(bf16), "z", pairs)
    return products[-1], arrived[0], arrived[1]


def line_gather(block, count):
    blocks = {0: block}
    up = down = block
    for step in range(1, count):
        up = lax.ppermute(up, "z", [(i, i + 1) for i in range(step - 1, count - 1)])
        down = lax.ppermute(down, "z", [(i, i - 1) for i in range(1, count - step + 1)])
        blocks[-step], blocks[step] = up, down
    return blocks


def blend_kernel(widths, place_ref, *refs):
    count = len(widths)
    teachers, students = refs[:count], refs[count : 2 * count]
    nexts, lows = refs[2 * count : 3 * count], refs[3 * count :]
    step = pl.program_id(0)
    start = 0
    for teacher, student, following, width in zip(teachers, students, nexts, widths):
        value = blend_keep * teacher[...] + (1.0 - blend_keep) * student[...]
        following[...] = value
        for bits, low in enumerate(lows):

            @pl.when(step == bits)
            def _(low=low, value=value, start=start, width=width):
                low[:, start : start + width] = value.astype(bf16)

        start += width


def blend(teachers, students, place, count):
    height = teachers[0].shape[0]
    widths = [x.shape[1] // count for x in teachers]
    columns = [
        pl.BlockSpec((height, width), lambda i, ref: (0, jnp.bitwise_xor(i, ref[0])))
        for width in widths
    ]
    low = pl.BlockSpec((height, sum(widths)), lambda i, ref: (0, 0))
    results = pl.pallas_call(
        functools.partial(blend_kernel, widths),
        grid_spec=pltpu.PrefetchScalarGridSpec(
            num_scalar_prefetch=1,
            grid=(count,),
            in_specs=columns * 2,
            out_specs=columns + [low] * count,
        ),
        out_shape=[jax.ShapeDtypeStruct(x.shape, f32) for x in teachers]
        + [jax.ShapeDtypeStruct((height, sum(widths)), bf16)] * count,
        compiler_params=pltpu.CompilerParams(vmem_limit_bytes=VMEM),
        cost_estimate=pl.CostEstimate(
            flops=3 * height * sum(widths) * count,
            bytes_accessed=14 * height * sum(widths) * count,
            transcendentals=0,
        ),
    )(place.reshape(1).astype(jnp.int32), *teachers, *students)
    return results[: len(teachers)], results[len(teachers) :]


def normalize_kernel(planes, core_ref, choose_ref, landed_ref, gain_ref, raw_ref, normed_ref):
    sources, blocks, slots, width = landed_ref.shape
    plane = normed_ref.shape[2]
    half = plane // CORES
    square = None
    for block in range(blocks):
        rows = landed_ref[:, block].astype(f32).reshape(sources * slots, width).astype(bf16)
        values = jnp.dot(choose_ref[...], rows, preferred_element_type=f32)
        raw_ref[block] = values.astype(bf16)
        part = jnp.sum(values * values, axis=1, keepdims=True)
        square = part if square is None else square + part
    scale = lax.rsqrt(square / (blocks * width) + norm_epsilon)
    core = core_ref[0]
    for first in range(0, blocks * width, half):
        block, start = first // width, first % width
        at = first // plane
        values = raw_ref[block, :, start : start + half].astype(f32)
        values = (values * scale * gain_ref[:, first : first + half]).astype(bf16)
        side = jnp.bitwise_xor(first % plane // half, core) * half
        normed_ref[at, :, pl.ds(pl.multiple_of(side, half), half)] = values


def normalize(choose, landed, gain, core_at, planes):
    rows = choose.shape[0]
    _, blocks, _, width = landed.shape
    return pl.pallas_call(
        functools.partial(normalize_kernel, planes),
        in_specs=[pl.BlockSpec(memory_space=pltpu.SMEM)]
        + [pl.BlockSpec(memory_space=pltpu.VMEM)] * 3,
        out_specs=[pl.BlockSpec(memory_space=pltpu.VMEM)] * 2,
        out_shape=[
            jax.ShapeDtypeStruct((blocks, rows, width), bf16),
            jax.ShapeDtypeStruct((planes, rows, blocks * width // planes), bf16),
        ],
        compiler_params=pltpu.CompilerParams(vmem_limit_bytes=VMEM),
        cost_estimate=pl.CostEstimate(
            flops=2 * rows * landed.size, bytes_accessed=4 * landed.size, transcendentals=0
        ),
    )(core_at.reshape(1).astype(jnp.int32), choose, landed, gain.reshape(1, -1))


def place_kernel(count, turned, place_ref, *refs):
    out_ref = refs[-1]
    height = refs[0].shape[0]
    for bits in range(count):
        at = jnp.bitwise_xor(place_ref[0], bits) * height
        at = pl.ds(pl.multiple_of(at, height), height)
        if turned:
            out_ref[:, at] = refs[bits][...].T
        else:
            out_ref[at, :] = refs[bits][...]


def in_order(by_bits, place, turned=False):
    count = len(by_bits)
    height, width = by_bits[0].shape
    shape = (width, count * height) if turned else (count * height, width)
    if turned and height % HEAD_WIDTH != 0:
        rows = [
            lax.dynamic_index_in_dim(
                jnp.stack(by_bits), jnp.bitwise_xor(place, i), 0, keepdims=False
            )
            for i in range(count)
        ]
        return jnp.concatenate(rows, axis=0).T
    return pl.pallas_call(
        functools.partial(place_kernel, count, turned),
        in_specs=[pl.BlockSpec(memory_space=pltpu.SMEM)]
        + [pl.BlockSpec(memory_space=pltpu.VMEM)] * count,
        out_specs=pl.BlockSpec(memory_space=pltpu.VMEM),
        out_shape=jax.ShapeDtypeStruct(shape, bf16),
        compiler_params=pltpu.CompilerParams(vmem_limit_bytes=VMEM),
        cost_estimate=pl.CostEstimate(
            flops=0, bytes_accessed=4 * count * height * width, transcendentals=0
        ),
    )(place.reshape(1).astype(jnp.int32), *by_bits)


def multiply_kernel(parts, *refs):
    rows, (mine_ref, other_ref, out_ref, all_ref) = refs[:parts], refs[parts:]
    height = rows[0].shape[0]
    depth = mine_ref.shape[0]

    @pl.when(pl.program_id(0) == 0)
    def _():
        for i, part in enumerate(rows):
            all_ref[i * height : (i + 1) * height, :] = part[...]

    product = jnp.dot(all_ref[:, :depth], mine_ref[...], preferred_element_type=f32)
    product += jnp.dot(all_ref[:, depth:], other_ref[...], preferred_element_type=f32)
    out_ref[...] = product.astype(out_ref.dtype)


def multiply(parts, mine, other, kind):
    height, depth = parts[0].shape
    width = mine.shape[1]
    tile = 512 if width % 512 == 0 else 128
    rows = pl.BlockSpec((height, depth), lambda i: (0, 0))
    weights = pl.BlockSpec((depth // CORES, tile), lambda i: (0, i))
    count = len(parts)
    return pl.pallas_call(
        functools.partial(multiply_kernel, count),
        grid=(width // tile,),
        in_specs=[rows] * count + [weights] * 2,
        out_specs=pl.BlockSpec((count * height, tile), lambda i: (0, i)),
        out_shape=jax.ShapeDtypeStruct((count * height, width), kind),
        scratch_shapes=[pltpu.VMEM((count * height, depth), bf16)],
        compiler_params=pltpu.CompilerParams(vmem_limit_bytes=24 * 1024 * 1024),
        cost_estimate=pl.CostEstimate(
            flops=2 * count * height * depth * width,
            bytes_accessed=2 * depth * width,
            transcendentals=0,
        ),
    )(*parts, mine, other)


def finish_kernel(
    turned_blocks, query_blocks, own_ref, up_ref, down_ref, cosine_ref, sine_ref, back_ref,
    query_ref, fresh_ref,
):
    wide = own_ref.shape[1] // HEAD_WIDTH
    first = pl.program_id(0) * wide
    values = own_ref[...] + up_ref[...].astype(f32) + down_ref[...].astype(f32)
    pieces = []
    for head in range(wide):
        piece = values[:, head * HEAD_WIDTH : (head + 1) * HEAD_WIDTH]
        rolled = pltpu.roll(piece, HEAD_WIDTH // 2, 1)
        turned = piece * cosine_ref[...] + rolled * sine_ref[...]
        pieces.append(jnp.where(first + head < turned_blocks, turned, piece).astype(bf16))
    values = jnp.concatenate(pieces, axis=1)
    values = jnp.dot(back_ref[...], values, preferred_element_type=f32).astype(bf16)

    @pl.when(first < query_blocks)
    def _():
        for head in range(wide):
            query_ref[head] = values[:, head * HEAD_WIDTH : (head + 1) * HEAD_WIDTH]

    @pl.when(first >= query_blocks)
    def _():
        fresh_ref[...] = values


def finish_projection(own, up, down, cosine_table, sine_table, back, query_blocks, key_blocks):
    tokens, width = own.shape
    blocks = width // HEAD_WIDTH
    wide = max(w for w in (1, 2, 4) if query_blocks % w == 0 and (blocks - query_blocks) % w == 0)
    column = pl.BlockSpec((tokens, wide * HEAD_WIDTH), lambda i: (0, i))
    table = pl.BlockSpec((tokens, HEAD_WIDTH), lambda i: (0, 0))
    steps = query_blocks // wide
    return pl.pallas_call(
        functools.partial(finish_kernel, query_blocks + key_blocks, query_blocks),
        grid=(blocks // wide,),
        in_specs=[column, column, column, table, table]
        + [pl.BlockSpec((tokens, tokens), lambda i: (0, 0))],
        out_specs=[
            pl.BlockSpec((wide, tokens, HEAD_WIDTH), lambda i: (jnp.minimum(i, steps - 1), 0, 0)),
            pl.BlockSpec((tokens, wide * HEAD_WIDTH), lambda i: (0, jnp.maximum(i - steps, 0))),
        ],
        out_shape=[
            jax.ShapeDtypeStruct((query_blocks, tokens, HEAD_WIDTH), bf16),
            jax.ShapeDtypeStruct((tokens, (blocks - query_blocks) * HEAD_WIDTH), bf16),
        ],
        compiler_params=pltpu.CompilerParams(vmem_limit_bytes=VMEM),
        cost_estimate=pl.CostEstimate(
            flops=2 * tokens * tokens * width,
            bytes_accessed=10 * tokens * width,
            transcendentals=0,
        ),
    )(own, up, down, cosine_table, sine_table, back)


def attend_kernel(rows, groups, lengths_ref, q_ref, fresh_ref, k_ref, v_ref, out_ref, total_ref):
    first = pl.program_id(0) * rows
    heads = q_ref.shape[0]
    slots, width = k_ref.shape[1], k_ref.shape[2]
    steps = DECODE_STEPS
    pair = 2 * steps
    height = heads * pair
    scale = HEAD_WIDTH ** (-0.5)
    contract_last = (((1,), (1,)), ((), ()))
    contract_mid = (((1,), (0,)), ((), ()))
    fresh_k = fresh_ref[:, :width]
    fresh_v = fresh_ref[:, width:]
    pairs = rows // 2
    queries = q_ref[...].astype(f32)
    band = height // groups
    wide = []
    for p in range(pairs):
        query = queries[:, p * pair : (p + 1) * pair, :].reshape(height, HEAD_WIDTH)
        if groups > 1:
            row_band = lax.broadcasted_iota(jnp.int32, (height, HEAD_WIDTH), 0) // band
            query = jnp.concatenate(
                [jnp.where(row_band == g, query, 0.0) for g in range(groups)], axis=1
            )
        wide.append(query.astype(bf16))
    second = (lax.broadcasted_iota(jnp.int32, (height, 1), 0) % pair) >= steps
    slot_index = lax.broadcasted_iota(jnp.int32, (height, slots), 1)
    fresh_index = lax.broadcasted_iota(jnp.int32, (height, rows * steps), 1)
    token_of = lax.broadcasted_iota(jnp.int32, (height, rows * steps), 0) % pair
    cached_scores, fresh_scores = [], []
    for p in range(pairs):
        one = lax.dot_general(wide[p], k_ref[2 * p], contract_last, preferred_element_type=f32)
        two = lax.dot_general(wide[p], k_ref[2 * p + 1], contract_last, preferred_element_type=f32)
        length = jnp.where(
            second, lengths_ref[first + 2 * p + 1], lengths_ref[first + 2 * p]
        )
        scores = jnp.where(second, two, one) * scale
        cached_scores.append(jnp.where(slot_index < length, scores, masked_score))
        fresh = lax.dot_general(wide[p], fresh_k, contract_last, preferred_element_type=f32)
        token = token_of + p * pair
        valid = (fresh_index // steps == token // steps) & (fresh_index <= token)
        fresh_scores.append(jnp.where(valid, fresh * scale, masked_score))
    for p in range(pairs):
        cached, fresh = cached_scores[p], fresh_scores[p]
        highest = jnp.maximum(
            jnp.max(cached, axis=-1, keepdims=True), jnp.max(fresh, axis=-1, keepdims=True)
        )
        cached = jnp.exp(cached - highest)
        fresh = jnp.exp(fresh - highest)
        totals = jnp.sum(cached, axis=-1, keepdims=True) + jnp.sum(fresh, axis=-1, keepdims=True)
        cached = cached / totals
        fresh = (fresh / totals).astype(bf16)
        attended = lax.dot_general(
            jnp.where(second, 0.0, cached).astype(bf16),
            v_ref[2 * p],
            contract_mid,
            preferred_element_type=f32,
        )
        attended += lax.dot_general(
            jnp.where(second, cached, 0.0).astype(bf16),
            v_ref[2 * p + 1],
            contract_mid,
            preferred_element_type=f32,
        )
        attended += lax.dot_general(fresh, fresh_v, contract_mid, preferred_element_type=f32)
        for head in range(heads):
            group = head * groups // heads
            total_ref[p * pair : (p + 1) * pair, head * HEAD_WIDTH : (head + 1) * HEAD_WIDTH] = (
                attended[
                    head * pair : (head + 1) * pair,
                    group * HEAD_WIDTH : (group + 1) * HEAD_WIDTH,
                ]
            )
    out_ref[...] = total_ref[...].astype(bf16)


def attend(queries, fresh, key_cache, value_cache, lengths):
    heads, tokens = queries.shape[0], queries.shape[1]
    row_count, slots, width = key_cache.shape
    groups = width // HEAD_WIDTH
    rows = 8
    held = rows * DECODE_STEPS
    return pl.pallas_call(
        functools.partial(attend_kernel, rows, groups),
        grid=(row_count // rows,),
        in_specs=[
            pl.BlockSpec(memory_space=pltpu.SMEM),
            pl.BlockSpec((heads, held, HEAD_WIDTH), lambda i: (0, i, 0)),
            pl.BlockSpec((held, 2 * width), lambda i: (i, 0)),
            pl.BlockSpec((rows, slots, width), lambda i: (i, 0, 0)),
            pl.BlockSpec((rows, slots, width), lambda i: (i, 0, 0)),
        ],
        out_specs=pl.BlockSpec((held, heads * HEAD_WIDTH), lambda i: (i, 0)),
        out_shape=jax.ShapeDtypeStruct((tokens, heads * HEAD_WIDTH), bf16),
        scratch_shapes=[pltpu.VMEM((held, heads * HEAD_WIDTH), f32)],
        compiler_params=pltpu.CompilerParams(vmem_limit_bytes=VMEM),
        cost_estimate=pl.CostEstimate(
            flops=8 * tokens * heads * slots * width,
            bytes_accessed=4 * row_count * slots * width,
            transcendentals=tokens * heads * slots,
        ),
    )(lengths, queries, fresh, key_cache, value_cache)


def term_kernel(places, info_ref, own_ref, other_ref, *refs):
    blocks = refs[: len(places)]
    own_out_ref, other_out_ref, weights_ref, arrival = refs[len(places) :]
    for place, block in zip(places, blocks):

        @pl.when(info_ref[0] == place)
        def _(block=block):
            copy = pltpu.make_async_copy(block, weights_ref, arrival)
            copy.start()
            copy.wait()

    weights = weights_ref[...]
    for rows_ref, out_ref in ((own_ref, own_out_ref), (other_ref, other_out_ref)):
        product = jnp.dot(rows_ref[...], weights, preferred_element_type=f32)
        out_ref[...] = product.astype(out_ref.dtype)


def term(own, other, blocks, place, own_type, other_type):
    places = sorted(blocks)
    depth, height = blocks[0].shape
    tokens = own.shape[0]
    whole = pl.BlockSpec(memory_space=pltpu.VMEM)
    return pl.pallas_call(
        functools.partial(term_kernel, places),
        in_specs=[pl.BlockSpec(memory_space=pltpu.SMEM), whole, whole]
        + [pl.BlockSpec(memory_space=pl.ANY)] * len(places),
        out_specs=[whole, whole],
        out_shape=[
            jax.ShapeDtypeStruct((tokens, height), own_type),
            jax.ShapeDtypeStruct((tokens, height), other_type),
        ],
        scratch_shapes=[pltpu.VMEM((depth, height), bf16), pltpu.SemaphoreType.DMA],
        compiler_params=pltpu.CompilerParams(vmem_limit_bytes=VMEM),
        cost_estimate=pl.CostEstimate(
            flops=4 * tokens * height * depth,
            bytes_accessed=2 * height * depth + 12 * tokens * height,
            transcendentals=0,
        ),
    )(place.reshape(1).astype(jnp.int32), own, other, *[blocks[p] for p in places])


def sum_over_tensor(attended, blocks, t_at, z_at, core_at, count):
    other = lax.ppermute(attended, "core", [(0, 1), (1, 0)])

    def of(bits, own_type, other_type):
        place = jnp.bitwise_xor(t_at, bits) - z_at
        return term(attended, other, blocks, place, own_type, other_type)

    if count == 4:
        far_own, far_other = of(3, bf16, bf16)
        far_own, far_other = swap(far_own, 1, count), swap(far_other, 2, count)
        near_own, pass_other = of(1, bf16, f32)
        near_own = swap(near_own, 1, count)
        pass_own, near_other = of(2, f32, bf16)
        near_other = swap(near_other, 2, count)
        pass_other = swap((pass_other + far_other.astype(f32)).astype(bf16), 1, count)
        pass_own = swap((pass_own + far_own.astype(f32)).astype(bf16), 2, count)
        sum_own, sum_other = of(0, f32, f32)
        sum_other = sum_other + near_other.astype(f32) + pass_other.astype(f32)
        sum_own = sum_own + near_own.astype(f32) + pass_own.astype(f32)
    else:
        terms = [
            term(attended, other, blocks, jnp.int32(b) - z_at, bf16, bf16) for b in range(count)
        ]
        sum_own, sum_other = (
            lax.psum_scatter(
                jnp.concatenate(rows, axis=1), "tensor", scatter_dimension=1, tiled=True
            ).astype(f32)
            for rows in zip(*terms)
        )
    came = lax.ppermute(sum_other.astype(bf16), "core", [(0, 1), (1, 0)]).astype(f32)
    return jnp.where(
        core_at == 0,
        jnp.concatenate([sum_own, came], axis=1),
        jnp.concatenate([came, sum_own], axis=1),
    )


def body(
    n_z,
    n_t,
    token_ids,
    cache_lengths,
    embedding,
    norm_gain,
    rotated_key_cache,
    stored_value_cache,
    teacher_q,
    teacher_k,
    teacher_v,
    teacher_o,
    student_q,
    student_k,
    student_v,
    student_o,
):
    n_r = n_z * CORES
    z_at, core_at, t_at = (lax.axis_index(name) for name in ("z", "core", "tensor"))
    rows, steps = token_ids.shape
    tokens = rows * steps
    shard_rows, feature_block = embedding.shape
    capacity = 2 * tokens // n_r
    quarter_slots = capacity // n_t
    quarter = tokens // n_t

    ids = token_ids.reshape(tokens)
    owner = ids // shard_rows
    is_owner = (owner[:, None] == jnp.arange(n_r)[None, :]).astype(jnp.int32)
    before = jnp.cumsum(is_owner, axis=0) - is_owner
    rank = jnp.sum(before * is_owner, axis=1)
    counts = jnp.sum(is_owner, axis=0)
    starts = jnp.cumsum(counts) - counts
    place = jnp.sum(is_owner * starts[None, :], axis=1) + rank
    part, spot = place % n_t, place // n_t
    slot = rank // n_t
    request_at = (owner * n_t + part) * quarter_slots + slot
    wanted = jnp.sum(
        jnp.where(
            request_at[None, :] == jnp.arange(n_r * capacity)[:, None],
            (ids - owner * shard_rows)[None, :],
            0,
        ),
        axis=1,
    ).reshape(n_r, capacity)
    asked = lax.all_to_all(wanted, ("z", "core"), 0, 0, tiled=True)

    (next_q, next_k, next_v), qkv_columns = blend(
        (teacher_q, teacher_k, teacher_v), (student_q, student_k, student_v), t_at, n_t
    )
    (next_o,), o_columns = blend((teacher_o,), (student_o,), t_at, n_t)
    qkv_by_bits = [x if b == 0 else swap(x, b, n_t) for b, x in enumerate(qkv_columns)]

    weights = in_order(qkv_by_bits, t_at)
    other = lax.ppermute(weights, "core", [(0, 1), (1, 0)])

    asked = after(asked, qkv_columns[-1])
    picked = jnp.take(embedding, asked.reshape(-1), axis=0, mode="clip")
    picked = picked.reshape(n_r * n_t, quarter_slots, feature_block)
    landed = lax.all_to_all(picked, ("z", "core", "tensor"), 0, 0, tiled=True)
    mine = (part == t_at)[None, :] & (spot[None, :] == jnp.arange(quarter)[:, None])
    source = jnp.sum(jnp.where(mine, (owner * quarter_slots + slot)[None, :], 0), axis=1)
    choose = (source[:, None] == jnp.arange(n_r * quarter_slots)[None, :]).astype(bf16)
    landed = landed.reshape(n_r, n_t, quarter_slots, feature_block)
    for columns in qkv_by_bits[1:]:
        choose = after(choose, columns)
    raw, normed = normalize(choose, landed, norm_gain, core_at, n_z)
    held = lax.all_to_all(normed, "z", 0, 0, tiled=True)

    o_by_bits = [
        x if b == 0 else swap(after(x, normed), b, n_t) for b, x in enumerate(o_columns)
    ]
    rows_o = in_order(o_by_bits, t_at, turned=True)

    order = jnp.asarray(due_order(n_z))[z_at]
    products = []
    for k in range(n_z):
        chunk = lax.dynamic_index_in_dim(held, order[k], 0, keepdims=False)
        if k == 0:
            for columns in o_by_bits[1:]:
                chunk = after(chunk, columns)
        chunk = [chunk] + [swap(chunk, b, n_t) for b in range(1, n_t)]
        last = chunk[-1]
        products.append(multiply(chunk, weights, other, f32 if k == n_z - 1 else bf16))
    blocks_o = line_gather(after(rows_o, held), n_z)
    gates = [blocks_o[-step] for step in range(1, n_z)]
    own, up, down = line_sum(products, z_at, n_z, gates)

    raw = after(raw, last)
    raw_by_bits = []
    for b in range(n_t):
        block = lax.dynamic_index_in_dim(raw, jnp.bitwise_xor(t_at, b), 0, keepdims=False)
        raw_by_bits.append(block if b == 0 else swap(block, b, n_t))
    residual = jnp.concatenate(raw_by_bits, axis=0)

    column = jnp.bitwise_xor(part, t_at) * quarter + spot
    back = column[:, None] == jnp.arange(tokens)[None, :]
    positions = (cache_lengths[:, None] + jnp.arange(steps, dtype=jnp.int32)[None, :]).reshape(-1)
    moved = jnp.sum(jnp.where(back, positions[:, None], 0), axis=0).astype(f32)
    inverse = rope_theta ** (-(jnp.arange(HEAD_WIDTH // 2, dtype=f32) * 2.0) / HEAD_WIDTH)
    angles = moved[:, None] * inverse
    cosine_table, sine_table = jnp.cos(angles), jnp.sin(angles)
    cosine_table = jnp.concatenate([cosine_table, cosine_table], axis=1)
    sine_table = jnp.concatenate([-sine_table, sine_table], axis=1)
    back = after(after(back.astype(bf16), blocks_o[1 - n_z]), blocks_o[n_z - 1])
    residual = jnp.dot(back, residual, preferred_element_type=f32)

    q_width = teacher_q.shape[1] // n_t
    k_width = teacher_k.shape[1] // n_t
    queries, fresh = finish_projection(
        own,
        up,
        down,
        cosine_table,
        sine_table,
        back,
        q_width // HEAD_WIDTH,
        k_width // HEAD_WIDTH,
    )
    attended = attend(queries, fresh, rotated_key_cache, stored_value_cache, cache_lengths)

    hidden = residual + sum_over_tensor(
        attended, blocks_o, t_at, z_at, core_at, n_t
    )
    hidden_out = hidden.astype(bf16).reshape(rows, steps, feature_block)
    return (next_q, next_k, next_v, next_o, hidden_out)


def solution(mesh):
    n_z = mesh.shape["replica"] // CORES
    n_t = mesh.shape["tensor"]
    split = jax.sharding.Mesh(mesh.devices.reshape(n_z, CORES, n_t), ("z", "core", "tensor"))
    replica = ("z", "core")
    every = ("z", "core", "tensor")
    return jax.shard_map(
        functools.partial(body, n_z, n_t),
        mesh=split,
        in_specs=(
            P(replica, None),
            P(replica),
            P(replica, "tensor"),
            P(),
            P(replica, None, "tensor"),
            P(replica, None, "tensor"),
        )
        + (P(every, None),) * 8,
        out_specs=(P(every, None),) * 4 + (P(replica, None, "tensor"),),
        check_vma=False,
    )
```

```python
import functools

import jax
import jax.numpy as jnp
import numpy as np
from jax import lax
from jax.experimental import pallas as pl
from jax.experimental.pallas import tpu as pltpu
from jax.sharding import PartitionSpec as P

D = 8192
HEAD_WIDTH = 128
DECODE_STEPS = 4
CORES = 2

blend_keep = 0.9
norm_epsilon = 1e-05
rope_theta = 500000.0
masked_score = -1e30

VMEM = 60 * 1024 * 1024

f32 = jnp.float32
bf16 = jnp.bfloat16


def swap(values, bits, count):
    return lax.ppermute(values, "tensor", [(i, i ^ bits) for i in range(count)])


def pass_kernel(values_ref, other_ref, out_ref):
    pass


def after(values, other):
    anywhere = pl.BlockSpec(memory_space=pl.ANY)
    return pl.pallas_call(
        pass_kernel,
        in_specs=[anywhere, anywhere],
        out_specs=anywhere,
        out_shape=jax.ShapeDtypeStruct(values.shape, values.dtype),
        input_output_aliases={0: 0},
        cost_estimate=pl.CostEstimate(flops=0, bytes_accessed=0, transcendentals=0),
    )(values, other)


def due_order(count):
    if count == 4:
        order = [[3, 2, 1, 0], [0, 3, 2, 1], [3, 0, 1, 2], [0, 1, 2, 3]]
    else:
        order = [
            sorted(range(count), key=lambda d, z=z: (d == z, -abs(d - z))) for z in range(count)
        ]
    return np.array(order, dtype=np.int32)


def line_sum(products, place, count):
    if count == 4:
        first, second, third, own = products
        one = lax.ppermute(first, "z", [(0, 1), (3, 2)])
        block = (second.astype(f32) + one.astype(f32)).astype(bf16)
        up = lax.ppermute(block, "z", [(0, 1), (1, 2)])
        down = lax.ppermute(block, "z", [(3, 2), (2, 1)])
        rest = jnp.where(place == 2, first, third).astype(f32)
        block = (rest + up.astype(f32)).astype(bf16)
        up = lax.ppermute(block, "z", [(0, 1), (1, 2), (2, 3)])
        rest = jnp.where(place == 1, first, third).astype(f32)
        block = (rest + down.astype(f32)).astype(bf16)
        down = lax.ppermute(block, "z", [(3, 2), (2, 1), (1, 0)])
        return own, up, down
    order = due_order(count)
    arrived = [None, None]
    for step in range(1, count):
        for way, sign in enumerate((1, -1)):
            sources = [z for z in range(count) if 0 <= z + sign * (count - step) < count]
            picks = {z: int(np.where(order[z] == z + sign * (count - step))[0][0]) for z in sources}
            names = sorted(set(picks.values()))
            block = products[names[0]].astype(f32)
            for name in names[1:]:
                chosen = functools.reduce(
                    jnp.logical_or, [place == z for z in sources if picks[z] == name]
                )
                block = jnp.where(chosen, products[name].astype(f32), block)
            if arrived[way] is not None:
                block = block + arrived[way].astype(f32)
            pairs = [(z, z + sign) for z in sources if 0 <= z + sign < count]
            arrived[way] = lax.ppermute(block.astype(bf16), "z", pairs)
    return products[-1], arrived[0], arrived[1]


def pass_on(up, down, step, count):
    up = lax.ppermute(up, "z", [(i, i + 1) for i in range(step - 1, count - 1)])
    down = lax.ppermute(down, "z", [(i, i - 1) for i in range(1, count - step + 1)])
    return up, down


def blend_kernel(widths, place_ref, *refs):
    count = len(widths)
    teachers, students = refs[:count], refs[count : 2 * count]
    nexts, lows = refs[2 * count : 3 * count], refs[3 * count :]
    step = pl.program_id(0)
    start = 0
    for teacher, student, following, width in zip(teachers, students, nexts, widths):
        value = blend_keep * teacher[...] + (1.0 - blend_keep) * student[...]
        following[...] = value
        for bits, low in enumerate(lows):

            @pl.when(step == bits)
            def _(low=low, value=value, start=start, width=width):
                low[:, start : start + width] = value.astype(bf16)

        start += width


def blend(teachers, students, place, count):
    height = teachers[0].shape[0]
    widths = [x.shape[1] // count for x in teachers]
    columns = [
        pl.BlockSpec((height, width), lambda i, ref: (0, jnp.bitwise_xor(i, ref[0])))
        for width in widths
    ]
    low = pl.BlockSpec((height, sum(widths)), lambda i, ref: (0, 0))
    results = pl.pallas_call(
        functools.partial(blend_kernel, widths),
        grid_spec=pltpu.PrefetchScalarGridSpec(
            num_scalar_prefetch=1,
            grid=(count,),
            in_specs=columns * 2,
            out_specs=columns + [low] * count,
        ),
        out_shape=[jax.ShapeDtypeStruct(x.shape, f32) for x in teachers]
        + [jax.ShapeDtypeStruct((height, sum(widths)), bf16)] * count,
        compiler_params=pltpu.CompilerParams(vmem_limit_bytes=VMEM),
        cost_estimate=pl.CostEstimate(
            flops=3 * height * sum(widths) * count,
            bytes_accessed=14 * height * sum(widths) * count,
            transcendentals=0,
        ),
    )(place.reshape(1).astype(jnp.int32), *teachers, *students)
    return results[: len(teachers)], results[len(teachers) :]


def normalize_kernel(planes, core_ref, choose_ref, landed_ref, gain_ref, raw_ref, normed_ref):
    sources, blocks, slots, width = landed_ref.shape
    plane = normed_ref.shape[2]
    half = plane // CORES
    square = None
    for block in range(blocks):
        rows = landed_ref[:, block].astype(f32).reshape(sources * slots, width).astype(bf16)
        values = jnp.dot(choose_ref[...], rows, preferred_element_type=f32)
        raw_ref[block] = values.astype(bf16)
        part = jnp.sum(values * values, axis=1, keepdims=True)
        square = part if square is None else square + part
    scale = lax.rsqrt(square / (blocks * width) + norm_epsilon)
    core = core_ref[0]
    for first in range(0, blocks * width, half):
        block, start = first // width, first % width
        at = first // plane
        values = raw_ref[block, :, start : start + half].astype(f32)
        values = (values * scale * gain_ref[:, first : first + half]).astype(bf16)
        side = jnp.bitwise_xor(first % plane // half, core) * half
        normed_ref[at, :, pl.ds(pl.multiple_of(side, half), half)] = values


def normalize(choose, landed, gain, core_at, planes):
    rows = choose.shape[0]
    _, blocks, _, width = landed.shape
    return pl.pallas_call(
        functools.partial(normalize_kernel, planes),
        in_specs=[pl.BlockSpec(memory_space=pltpu.SMEM)]
        + [pl.BlockSpec(memory_space=pltpu.VMEM)] * 3,
        out_specs=[pl.BlockSpec(memory_space=pltpu.VMEM)] * 2,
        out_shape=[
            jax.ShapeDtypeStruct((blocks, rows, width), bf16),
            jax.ShapeDtypeStruct((planes, rows, blocks * width // planes), bf16),
        ],
        compiler_params=pltpu.CompilerParams(vmem_limit_bytes=VMEM),
        cost_estimate=pl.CostEstimate(
            flops=2 * rows * landed.size, bytes_accessed=4 * landed.size, transcendentals=0
        ),
    )(core_at.reshape(1).astype(jnp.int32), choose, landed, gain.reshape(1, -1))


def place_kernel(count, turned, place_ref, *refs):
    out_ref = refs[-1]
    height = refs[0].shape[0]
    for bits in range(count):
        at = jnp.bitwise_xor(place_ref[0], bits) * height
        at = pl.ds(pl.multiple_of(at, height), height)
        if turned:
            out_ref[:, at] = refs[bits][...].T
        else:
            out_ref[at, :] = refs[bits][...]


def in_order(by_bits, place, turned=False):
    count = len(by_bits)
    height, width = by_bits[0].shape
    shape = (width, count * height) if turned else (count * height, width)
    if turned and height % HEAD_WIDTH != 0:
        rows = [
            lax.dynamic_index_in_dim(
                jnp.stack(by_bits), jnp.bitwise_xor(place, i), 0, keepdims=False
            )
            for i in range(count)
        ]
        return jnp.concatenate(rows, axis=0).T
    return pl.pallas_call(
        functools.partial(place_kernel, count, turned),
        in_specs=[pl.BlockSpec(memory_space=pltpu.SMEM)]
        + [pl.BlockSpec(memory_space=pltpu.VMEM)] * count,
        out_specs=pl.BlockSpec(memory_space=pltpu.VMEM),
        out_shape=jax.ShapeDtypeStruct(shape, bf16),
        compiler_params=pltpu.CompilerParams(vmem_limit_bytes=VMEM),
        cost_estimate=pl.CostEstimate(
            flops=0, bytes_accessed=4 * count * height * width, transcendentals=0
        ),
    )(place.reshape(1).astype(jnp.int32), *by_bits)


def multiply_kernel(parts, *refs):
    rows, (mine_ref, other_ref, out_ref, all_ref) = refs[:parts], refs[parts:]
    height = rows[0].shape[0]
    depth = mine_ref.shape[0]

    @pl.when(pl.program_id(0) == 0)
    def _():
        for i, part in enumerate(rows):
            all_ref[i * height : (i + 1) * height, :] = part[...]

    product = jnp.dot(all_ref[:, :depth], mine_ref[...], preferred_element_type=f32)
    product += jnp.dot(all_ref[:, depth:], other_ref[...], preferred_element_type=f32)
    out_ref[...] = product.astype(out_ref.dtype)


def multiply(parts, mine, other, kind):
    height, depth = parts[0].shape
    width = mine.shape[1]
    tile = 512 if width % 512 == 0 else 128
    rows = pl.BlockSpec((height, depth), lambda i: (0, 0))
    weights = pl.BlockSpec((depth // CORES, tile), lambda i: (0, i))
    count = len(parts)
    return pl.pallas_call(
        functools.partial(multiply_kernel, count),
        grid=(width // tile,),
        in_specs=[rows] * count + [weights] * 2,
        out_specs=pl.BlockSpec((count * height, tile), lambda i: (0, i)),
        out_shape=jax.ShapeDtypeStruct((count * height, width), kind),
        scratch_shapes=[pltpu.VMEM((count * height, depth), bf16)],
        compiler_params=pltpu.CompilerParams(vmem_limit_bytes=24 * 1024 * 1024),
        cost_estimate=pl.CostEstimate(
            flops=2 * count * height * depth * width,
            bytes_accessed=2 * depth * width,
            transcendentals=0,
        ),
    )(*parts, mine, other)


def finish_kernel(
    turned_blocks, query_blocks, own_ref, up_ref, down_ref, cosine_ref, sine_ref, back_ref,
    query_ref, fresh_ref,
):
    wide = own_ref.shape[1] // HEAD_WIDTH
    first = pl.program_id(0) * wide
    values = own_ref[...] + up_ref[...].astype(f32) + down_ref[...].astype(f32)
    pieces = []
    for head in range(wide):
        piece = values[:, head * HEAD_WIDTH : (head + 1) * HEAD_WIDTH]
        rolled = pltpu.roll(piece, HEAD_WIDTH // 2, 1)
        turned = piece * cosine_ref[...] + rolled * sine_ref[...]
        pieces.append(jnp.where(first + head < turned_blocks, turned, piece).astype(bf16))
    values = jnp.concatenate(pieces, axis=1)
    values = jnp.dot(back_ref[...], values, preferred_element_type=f32).astype(bf16)

    @pl.when(first < query_blocks)
    def _():
        for head in range(wide):
            query_ref[head] = values[:, head * HEAD_WIDTH : (head + 1) * HEAD_WIDTH]

    @pl.when(first >= query_blocks)
    def _():
        fresh_ref[...] = values


def finish_projection(own, up, down, cosine_table, sine_table, back, query_blocks, key_blocks):
    tokens, width = own.shape
    blocks = width // HEAD_WIDTH
    wide = max(w for w in (1, 2, 4) if query_blocks % w == 0 and (blocks - query_blocks) % w == 0)
    column = pl.BlockSpec((tokens, wide * HEAD_WIDTH), lambda i: (0, i))
    table = pl.BlockSpec((tokens, HEAD_WIDTH), lambda i: (0, 0))
    steps = query_blocks // wide
    return pl.pallas_call(
        functools.partial(finish_kernel, query_blocks + key_blocks, query_blocks),
        grid=(blocks // wide,),
        in_specs=[column, column, column, table, table]
        + [pl.BlockSpec((tokens, tokens), lambda i: (0, 0))],
        out_specs=[
            pl.BlockSpec((wide, tokens, HEAD_WIDTH), lambda i: (jnp.minimum(i, steps - 1), 0, 0)),
            pl.BlockSpec((tokens, wide * HEAD_WIDTH), lambda i: (0, jnp.maximum(i - steps, 0))),
        ],
        out_shape=[
            jax.ShapeDtypeStruct((query_blocks, tokens, HEAD_WIDTH), bf16),
            jax.ShapeDtypeStruct((tokens, (blocks - query_blocks) * HEAD_WIDTH), bf16),
        ],
        compiler_params=pltpu.CompilerParams(vmem_limit_bytes=16 * 1024 * 1024),
        cost_estimate=pl.CostEstimate(
            flops=2 * tokens * tokens * width,
            bytes_accessed=10 * tokens * width,
            transcendentals=0,
        ),
    )(own, up, down, cosine_table, sine_table, back)


def attend_kernel(rows, groups, lengths_ref, q_ref, fresh_ref, k_ref, v_ref, out_ref, total_ref):
    first = pl.program_id(0) * rows
    heads = q_ref.shape[0]
    slots, width = k_ref.shape[1], k_ref.shape[2]
    steps = DECODE_STEPS
    pair = 2 * steps
    height = heads * pair
    scale = HEAD_WIDTH ** (-0.5)
    contract_last = (((1,), (1,)), ((), ()))
    contract_mid = (((1,), (0,)), ((), ()))
    fresh_k = fresh_ref[:, :width]
    fresh_v = fresh_ref[:, width:]
    pairs = rows // 2
    queries = q_ref[...].astype(f32)
    band = height // groups
    wide = []
    for p in range(pairs):
        query = queries[:, p * pair : (p + 1) * pair, :].reshape(height, HEAD_WIDTH)
        if groups > 1:
            row_band = lax.broadcasted_iota(jnp.int32, (height, HEAD_WIDTH), 0) // band
            query = jnp.concatenate(
                [jnp.where(row_band == g, query, 0.0) for g in range(groups)], axis=1
            )
        wide.append(query.astype(bf16))
    second = (lax.broadcasted_iota(jnp.int32, (height, 1), 0) % pair) >= steps
    slot_index = lax.broadcasted_iota(jnp.int32, (height, slots), 1)
    fresh_index = lax.broadcasted_iota(jnp.int32, (height, rows * steps), 1)
    token_of = lax.broadcasted_iota(jnp.int32, (height, rows * steps), 0) % pair
    cached_scores, fresh_scores = [], []
    for p in range(pairs):
        one = lax.dot_general(wide[p], k_ref[2 * p], contract_last, preferred_element_type=f32)
        two = lax.dot_general(wide[p], k_ref[2 * p + 1], contract_last, preferred_element_type=f32)
        length = jnp.where(
            second, lengths_ref[first + 2 * p + 1], lengths_ref[first + 2 * p]
        )
        scores = jnp.where(second, two, one) * scale
        cached_scores.append(jnp.where(slot_index < length, scores, masked_score))
        fresh = lax.dot_general(wide[p], fresh_k, contract_last, preferred_element_type=f32)
        token = token_of + p * pair
        valid = (fresh_index // steps == token // steps) & (fresh_index <= token)
        fresh_scores.append(jnp.where(valid, fresh * scale, masked_score))
    for p in range(pairs):
        cached, fresh = cached_scores[p], fresh_scores[p]
        highest = jnp.maximum(
            jnp.max(cached, axis=-1, keepdims=True), jnp.max(fresh, axis=-1, keepdims=True)
        )
        cached = jnp.exp(cached - highest)
        fresh = jnp.exp(fresh - highest)
        totals = jnp.sum(cached, axis=-1, keepdims=True) + jnp.sum(fresh, axis=-1, keepdims=True)
        cached = cached / totals
        fresh = (fresh / totals).astype(bf16)
        attended = lax.dot_general(
            jnp.where(second, 0.0, cached).astype(bf16),
            v_ref[2 * p],
            contract_mid,
            preferred_element_type=f32,
        )
        attended += lax.dot_general(
            jnp.where(second, cached, 0.0).astype(bf16),
            v_ref[2 * p + 1],
            contract_mid,
            preferred_element_type=f32,
        )
        attended += lax.dot_general(fresh, fresh_v, contract_mid, preferred_element_type=f32)
        for head in range(heads):
            group = head * groups // heads
            total_ref[p * pair : (p + 1) * pair, head * HEAD_WIDTH : (head + 1) * HEAD_WIDTH] = (
                attended[
                    head * pair : (head + 1) * pair,
                    group * HEAD_WIDTH : (group + 1) * HEAD_WIDTH,
                ]
            )
    out_ref[...] = total_ref[...].astype(bf16)


def attend(queries, fresh, key_cache, value_cache, lengths):
    heads, tokens = queries.shape[0], queries.shape[1]
    row_count, slots, width = key_cache.shape
    groups = width // HEAD_WIDTH
    rows = 16 if row_count % 16 == 0 else 8
    held = rows * DECODE_STEPS
    return pl.pallas_call(
        functools.partial(attend_kernel, rows, groups),
        grid=(row_count // rows,),
        in_specs=[
            pl.BlockSpec(memory_space=pltpu.SMEM),
            pl.BlockSpec((heads, held, HEAD_WIDTH), lambda i: (0, i, 0)),
            pl.BlockSpec((held, 2 * width), lambda i: (i, 0)),
            pl.BlockSpec((rows, slots, width), lambda i: (i, 0, 0)),
            pl.BlockSpec((rows, slots, width), lambda i: (i, 0, 0)),
        ],
        out_specs=pl.BlockSpec((held, heads * HEAD_WIDTH), lambda i: (i, 0)),
        out_shape=jax.ShapeDtypeStruct((tokens, heads * HEAD_WIDTH), bf16),
        scratch_shapes=[pltpu.VMEM((held, heads * HEAD_WIDTH), f32)],
        compiler_params=pltpu.CompilerParams(vmem_limit_bytes=VMEM),
        cost_estimate=pl.CostEstimate(
            flops=8 * tokens * heads * slots * width,
            bytes_accessed=4 * row_count * slots * width,
            transcendentals=tokens * heads * slots,
        ),
    )(lengths, queries, fresh, key_cache, value_cache)


def term_kernel(places, info_ref, own_ref, other_ref, *refs):
    blocks = refs[: len(places)]
    own_out_ref, other_out_ref, weights_ref, arrival = refs[len(places) :]
    step = pl.program_id(0)
    for place, block in zip(places, blocks):

        @pl.when((info_ref[0] == place) & (step == 0))
        def _(block=block):
            copy = pltpu.make_async_copy(block, weights_ref, arrival)
            copy.start()
            copy.wait()

    for at, rows_ref, out_ref in ((0, own_ref, own_out_ref), (1, other_ref, other_out_ref)):

        @pl.when(step == at)
        def _(rows_ref=rows_ref, out_ref=out_ref):
            product = jnp.dot(rows_ref[...], weights_ref[...], preferred_element_type=f32)
            out_ref[...] = product.astype(out_ref.dtype)


def term(own, other, blocks, place, own_type, other_type):
    places = sorted(blocks)
    depth, height = blocks[0].shape
    tokens = own.shape[0]
    rows = pl.BlockSpec((tokens, depth), lambda i: (0, 0))
    sums = pl.BlockSpec((tokens, height), lambda i: (0, 0))
    return pl.pallas_call(
        functools.partial(term_kernel, places),
        grid=(2,),
        in_specs=[pl.BlockSpec(memory_space=pltpu.SMEM), rows, rows]
        + [pl.BlockSpec(memory_space=pl.ANY)] * len(places),
        out_specs=[sums, sums],
        out_shape=[
            jax.ShapeDtypeStruct((tokens, height), own_type),
            jax.ShapeDtypeStruct((tokens, height), other_type),
        ],
        scratch_shapes=[pltpu.VMEM((depth, height), bf16), pltpu.SemaphoreType.DMA],
        compiler_params=pltpu.CompilerParams(vmem_limit_bytes=24 * 1024 * 1024),
        cost_estimate=pl.CostEstimate(
            flops=4 * tokens * height * depth,
            bytes_accessed=2 * height * depth + 12 * tokens * height,
            transcendentals=0,
        ),
    )(place.reshape(1).astype(jnp.int32), own, other, *[blocks[p] for p in places])


def sum_over_tensor(attended, blocks, t_at, z_at, core_at, count):
    other = lax.ppermute(attended, "core", [(0, 1), (1, 0)])

    def of(bits, own_type, other_type, own=attended, other=other):
        place = jnp.bitwise_xor(t_at, bits) - z_at
        return term(own, other, blocks, place, own_type, other_type)

    if count == 4:
        far_own, far_other = of(3, bf16, bf16)
        far_own, far_other = swap(far_own, 1, count), swap(far_other, 2, count)
        near_own, pass_other = of(1, bf16, f32)
        near_own = swap(near_own, 1, count)
        pass_own, near_other = of(2, f32, bf16)
        near_other = swap(near_other, 2, count)
        pass_other = swap((pass_other + far_other.astype(f32)).astype(bf16), 1, count)
        pass_own = swap((pass_own + far_own.astype(f32)).astype(bf16), 2, count)
        sum_own, sum_other = of(0, f32, f32, after(attended, near_own), after(other, near_other))
        sum_other = sum_other + near_other.astype(f32) + pass_other.astype(f32)
        sum_own = sum_own + near_own.astype(f32) + pass_own.astype(f32)
    else:
        terms = [
            term(attended, other, blocks, jnp.int32(b) - z_at, bf16, bf16) for b in range(count)
        ]
        sum_own, sum_other = (
            lax.psum_scatter(
                jnp.concatenate(rows, axis=1), "tensor", scatter_dimension=1, tiled=True
            ).astype(f32)
            for rows in zip(*terms)
        )
    came = lax.ppermute(sum_other.astype(bf16), "core", [(0, 1), (1, 0)]).astype(f32)
    return jnp.where(
        core_at == 0,
        jnp.concatenate([sum_own, came], axis=1),
        jnp.concatenate([came, sum_own], axis=1),
    )


def body(
    n_z,
    n_t,
    token_ids,
    cache_lengths,
    embedding,
    norm_gain,
    rotated_key_cache,
    stored_value_cache,
    teacher_q,
    teacher_k,
    teacher_v,
    teacher_o,
    student_q,
    student_k,
    student_v,
    student_o,
):
    n_r = n_z * CORES
    z_at, core_at, t_at = (lax.axis_index(name) for name in ("z", "core", "tensor"))
    rows, steps = token_ids.shape
    tokens = rows * steps
    shard_rows, feature_block = embedding.shape
    capacity = 2 * tokens // n_r
    quarter_slots = capacity // n_t
    quarter = tokens // n_t

    ids = token_ids.reshape(tokens)
    owner = ids // shard_rows
    is_owner = (owner[:, None] == jnp.arange(n_r)[None, :]).astype(jnp.int32)
    before = jnp.cumsum(is_owner, axis=0) - is_owner
    rank = jnp.sum(before * is_owner, axis=1)
    counts = jnp.sum(is_owner, axis=0)
    starts = jnp.cumsum(counts) - counts
    place = jnp.sum(is_owner * starts[None, :], axis=1) + rank
    part, spot = place % n_t, place // n_t
    slot = rank // n_t
    request_at = (owner * n_t + part) * quarter_slots + slot
    wanted = jnp.sum(
        jnp.where(
            request_at[None, :] == jnp.arange(n_r * capacity)[:, None],
            (ids - owner * shard_rows)[None, :],
            0,
        ),
        axis=1,
    ).reshape(n_r, capacity)
    asked = lax.all_to_all(wanted, ("z", "core"), 0, 0, tiled=True)

    (next_o,), o_columns = blend((teacher_o,), (student_o,), t_at, n_t)
    (next_q, next_k, next_v), qkv_columns = blend(
        (teacher_q, teacher_k, teacher_v), (student_q, student_k, student_v), t_at, n_t
    )
    o_by_bits = [x if b == 0 else swap(x, b, n_t) for b, x in enumerate(o_columns)]

    asked = after(asked, o_columns[-1])
    picked = jnp.take(embedding, asked.reshape(-1), axis=0, mode="clip")
    picked = picked.reshape(n_r * n_t, quarter_slots, feature_block)
    landed = lax.all_to_all(picked, ("z", "core", "tensor"), 0, 0, tiled=True)
    mine = (part == t_at)[None, :] & (spot[None, :] == jnp.arange(quarter)[:, None])
    source = jnp.sum(jnp.where(mine, (owner * quarter_slots + slot)[None, :], 0), axis=1)
    choose = (source[:, None] == jnp.arange(n_r * quarter_slots)[None, :]).astype(bf16)
    landed = landed.reshape(n_r, n_t, quarter_slots, feature_block)
    column = jnp.bitwise_xor(part, t_at) * quarter + spot
    back = column[:, None] == jnp.arange(tokens)[None, :]
    positions = (cache_lengths[:, None] + jnp.arange(steps, dtype=jnp.int32)[None, :]).reshape(-1)
    moved = jnp.sum(jnp.where(back, positions[:, None], 0), axis=0).astype(f32)
    inverse = rope_theta ** (-(jnp.arange(HEAD_WIDTH // 2, dtype=f32) * 2.0) / HEAD_WIDTH)
    angles = moved[:, None] * inverse
    cosine_table, sine_table = jnp.cos(angles), jnp.sin(angles)
    cosine_table = jnp.concatenate([cosine_table, cosine_table], axis=1)
    sine_table = jnp.concatenate([-sine_table, sine_table], axis=1)

    rows_o = in_order(o_by_bits, t_at, turned=True)
    for earlier in (rows_o, cosine_table, sine_table, qkv_columns[0]):
        choose = after(choose, earlier)
    raw, normed = normalize(choose, landed, norm_gain, core_at, n_z)
    held = lax.all_to_all(normed, "z", 0, 0, tiled=True)

    qkv_by_bits = [
        x if b == 0 else swap(after(x, normed), b, n_t) for b, x in enumerate(qkv_columns)
    ]
    order = [
        sum(jnp.where(z_at == z, int(place), 0) for z, place in enumerate(column))
        for column in due_order(n_z).T
    ]
    chunks = [lax.dynamic_index_in_dim(held, place, 0, keepdims=False) for place in order]
    weights = in_order([after(qkv_by_bits[0], chunks[0])] + qkv_by_bits[1:], t_at)
    other = lax.ppermute(weights, "core", [(0, 1), (1, 0)])
    rows_o = after(rows_o, chunks[0])
    blocks_o = {0: rows_o}
    up_o, down_o = pass_on(rows_o, rows_o, 1, n_z)
    products = []
    for k in range(n_z):
        chunk = [chunks[k]] + [swap(chunks[k], b, n_t) for b in range(1, n_t)]
        last = chunk[-1]
        if k == n_z - 1:
            weights = after(after(weights, blocks_o[-2]), blocks_o[2])
        products.append(multiply(chunk, weights, other, f32 if k == n_z - 1 else bf16))
        if k == 0:
            up_o, down_o = after(up_o, products[0]), after(down_o, products[0])
            blocks_o[-1], blocks_o[1] = up_o, down_o
            for step in range(2, n_z):
                up_o, down_o = pass_on(up_o, down_o, step, n_z)
                blocks_o[-step], blocks_o[step] = up_o, down_o
    own, up, down = line_sum(products, z_at, n_z)

    raw = after(raw, last)
    raw_by_bits = []
    for b in range(n_t):
        block = lax.dynamic_index_in_dim(raw, jnp.bitwise_xor(t_at, b), 0, keepdims=False)
        raw_by_bits.append(block if b == 0 else swap(block, b, n_t))
    residual = jnp.concatenate(raw_by_bits, axis=0)

    back = after(after(back.astype(bf16), blocks_o[1 - n_z]), blocks_o[n_z - 1])
    residual = jnp.dot(back, residual, preferred_element_type=f32)

    q_width = teacher_q.shape[1] // n_t
    k_width = teacher_k.shape[1] // n_t
    queries, fresh = finish_projection(
        after(own, residual),
        up,
        down,
        cosine_table,
        sine_table,
        back,
        q_width // HEAD_WIDTH,
        k_width // HEAD_WIDTH,
    )
    attended = attend(queries, fresh, rotated_key_cache, stored_value_cache, cache_lengths)

    hidden = residual + sum_over_tensor(
        attended, blocks_o, t_at, z_at, core_at, n_t
    )
    hidden_out = hidden.astype(bf16).reshape(rows, steps, feature_block)
    return (next_q, next_k, next_v, next_o, hidden_out)


def solution(mesh):
    n_z = mesh.shape["replica"] // CORES
    n_t = mesh.shape["tensor"]
    split = jax.sharding.Mesh(mesh.devices.reshape(n_z, CORES, n_t), ("z", "core", "tensor"))
    replica = ("z", "core")
    every = ("z", "core", "tensor")
    return jax.shard_map(
        functools.partial(body, n_z, n_t),
        mesh=split,
        in_specs=(
            P(replica, None),
            P(replica),
            P(replica, "tensor"),
            P(),
            P(replica, None, "tensor"),
            P(replica, None, "tensor"),
        )
        + (P(every, None),) * 8,
        out_specs=(P(every, None),) * 4 + (P(replica, None, "tensor"),),
        check_vma=False,
    )
```
